1024 devices in a mesh: sect: 16 (over x_hi, z), blk: 64 (over x_lo, y, core).
Axes of the slice: x: 8 (x_hi: 2, x_lo: 4; x = x_hi * 4 + x_lo), y: 8, z: 8, core: 2. Of those that a mesh axis runs over, the one named last changes fastest.
Arguments:
- fields: float32 [5, 32, 512, 128], P(None, 'sect', 'blk'), may hold values from -6 to 6
- history: bfloat16 [246, 32, 512, 128], P(None, 'sect', 'blk'), may hold values from -800 to 800
- levels: int32 [16, 64], P('sect', 'blk'), may hold values from 0 to 1
- diffusivity: float32 [5], replicated, may hold values from 0.03 to 0.15
- coupling: float32 [5, 5], replicated, may hold values from -1.75 to 1.75
Outputs:
- pod_modes: float32 [256, 32, 512, 128], P(None, 'sect', 'blk')
- factor: float32 [256, 256], replicated
The draws below stay inside these ranges and needn't reach their ends.
All inputs are finite; a program needn't handle non-finite values.
Results may differ from the reference program's by a relative error of at most 0.0003.
Values sent between devices are 32-bit elements; how exact they have to be, the bound alone decides.
A program may use at most 128 MiB of HBM per device.

```python
import math
import jax
import jax.numpy as jnp
from jax import lax

F = 5
SNAP = 256
HIST = 246
CX = 2
CY = 8
NX = 32
NY = 512
NZ = 128
ROWS = 2097152
N_SECT = 16
N_BLK = 64


def draw_history(key, part):
    key = jax.random.fold_in(key, 7)
    keys = jax.random.split(key, 4)
    shape = (HIST, NX, NY, NZ)
    rising = 1.0 + 2.0 * lax.broadcasted_iota(jnp.float32, (1, 1, NY, 1), 2) / NY
    noise = jnp.clip(jax.random.normal(keys[0], shape, jnp.float32), -4.0, 4.0)
    row_scale = jnp.exp(jax.random.uniform(keys[2], (1, NX, NY, NZ), jnp.float32, 0.0, math.log(3.0)))
    col_scale = jnp.exp(jax.random.uniform(keys[3], (HIST, 1, 1, 1), jnp.float32, 0.0, math.log(3.0)))
    common = jnp.clip(jax.random.normal(keys[1], (1, NX, NY, NZ), jnp.float32), -4.0, 4.0)
    base = noise + 0.6 * jnp.roll(noise, 1, axis=0) + 0.5 * common
    return (0.3 * base * rising * row_scale * col_scale).astype(jnp.bfloat16)


def plant(values, stream_key, low, high):
    longest = values.shape.index(max(values.shape))
    spots = []
    for shift in (0, 1):
        where = [jax.random.randint(jax.random.fold_in(stream_key, axis), (), 0, length) for axis, length in enumerate(values.shape)]
        where[longest] = (where[longest] + shift) % values.shape[longest]
        spots.append(tuple(where))
    return values.at[spots[0]].set(low).at[spots[1]].set(high)


def block_scale(rng, dims, pieces, least, high):
    loudness, own = 1.0, jax.random.fold_in(rng, 6)
    for dim, parts in pieces:
        steps = jnp.exp(jax.random.uniform(jax.random.fold_in(own, dim), (parts,), jnp.float32, least / len(pieces), high / len(pieces)))
        loudness = loudness * jnp.repeat(steps, dims[dim] // parts).reshape([-1 if axis == dim else 1 for axis in range(len(dims))])
    return loudness


def centred(own_key, extent, spread, most, shards=(), kind=jnp.bfloat16):
    array = spread * jax.random.normal(own_key, extent, jnp.float32)
    if shards:
        array = array * block_scale(own_key, extent, shards, -0.22, 0.18)
    return jnp.clip(array, -most, most).astype(kind)


def setup_inputs(seed: int = 0) -> dict:
    seeds = jax.random.split(jax.random.key(seed), 6)
    return {
        "fields": centred(seeds[0], (F, NX, NY, NZ), 1.0, 6.0, ((1, 16), (2, 64)), jnp.float32),
        "history": draw_history(jax.random.fold_in(seeds[5], 71), 0),
        "levels": plant(jax.random.randint(seeds[2], (N_SECT, N_BLK), 0, 2), jax.random.fold_in(seeds[2], 1), 0, 1).astype(jnp.int32),
        "diffusivity": jnp.clip(jnp.exp(jax.random.uniform(seeds[3], (F,), jnp.float32, math.log(0.03), math.log(0.15))), 0.03, 0.15),
        "coupling": centred(seeds[4], (F, F), 0.3, 1.75, (), jnp.float32),
    }


def tendency(current, diffusivity, coupling):
    padded = jnp.pad(current, ((0, 0), (1, 1), (1, 1), (1, 1)))
    center = padded[:, 1:-1, 1:-1, 1:-1]
    beside_all = padded[:, 2:, 1:-1, 1:-1] + padded[:, :-2, 1:-1, 1:-1]
    beside_all = beside_all + padded[:, 1:-1, 2:, 1:-1] + padded[:, 1:-1, :-2, 1:-1]
    beside_all = beside_all + padded[:, 1:-1, 1:-1, 2:] + padded[:, 1:-1, 1:-1, :-2]
    beside_all = beside_all - 6.0 * center
    coupled = jnp.einsum('fg,gxyz->fxyz', coupling, current, precision=lax.Precision.HIGHEST)
    return diffusivity[:, None, None, None] * beside_all + coupled

def reference(fields, history, levels, diffusivity, coupling):
    refined = jnp.repeat(jnp.repeat(levels, CX, axis=0), CY, axis=1).astype(jnp.float32)[None, :, :, None]
    stride = 1.0 / (1.0 + refined)
    first_state = fields + stride * tendency(fields, diffusivity, coupling)
    final_state = first_state + refined * stride * tendency(first_state, diffusivity, coupling)
    change = final_state - fields
    fresh = jnp.concatenate([final_state, change], axis=0)

    def slab_rows(slab):
        slab = jnp.asarray(slab).astype(jnp.int32)
        stored = lax.dynamic_index_in_dim(history, slab, axis=1, keepdims=False).astype(jnp.float32)
        recent = lax.dynamic_index_in_dim(fresh, slab, axis=1, keepdims=False)
        return jnp.concatenate([stored, recent], axis=0).reshape(SNAP, NY * NZ)

    def add_slab(slab, gram_sum):
        block = slab_rows(slab)
        return gram_sum + jnp.dot(block, block.T, precision=lax.Precision.HIGHEST)
    gram_total = lax.fori_loop(0, NX, add_slab, jnp.zeros((SNAP, SNAP), jnp.float32))
    upper_tri = jnp.linalg.cholesky(gram_total).T
    factor = upper_tri / jnp.sqrt(jnp.float32(ROWS))
    lower_tri = factor.T

    def put_slab(slab, outcome):
        block = slab_rows(slab)
        solved = lax.linalg.triangular_solve(lower_tri, block, left_side=True, lower=True)
        return lax.dynamic_update_index_in_dim(outcome, solved.reshape(SNAP, NY, NZ), jnp.asarray(slab).astype(jnp.int32), 1)
    pod_modes = lax.fori_loop(0, NX, put_slab, jnp.zeros((SNAP, NX, NY, NZ), jnp.float32))
    return (pod_modes, factor)
```

```python
import functools
import math

import jax
import jax.numpy as jnp
from jax import lax
from jax.experimental import pallas as pl
from jax.experimental.pallas import tpu as pltpu
from jax.sharding import PartitionSpec as P

F32 = jnp.float32
BF16 = jnp.bfloat16
MESH = pl.DeviceIdType.MESH
Z_CHIPS = 8
Y_CHIPS = 8
X_LOW = 4
RING = 8
BLOCK = 32
GROUP = 16


def position():
    sect = lax.axis_index("sect")
    blk = lax.axis_index("blk")
    x = (sect // Z_CHIPS) * X_LOW + blk // (2 * Y_CHIPS)
    y = (blk // 2) % Y_CHIPS
    return x, y, sect % Z_CHIPS, blk % 2


def device(x, y, z, core):
    return ((x // X_LOW) * Z_CHIPS + z, ((x % X_LOW) * Y_CHIPS + y) * 2 + core)


def neighbour_sum(cells, sect_low, sect_high, blk_low, blk_high, sub, lane):
    out = []
    for f in range(len(cells)):
        row = []
        for x in range(2):
            c = cells[f][x]
            low = sect_low[f] if x == 0 else cells[f][0]
            high = sect_high[f] if x == 1 else cells[f][1]
            up = jnp.where(sub == 0, jnp.broadcast_to(blk_low[2 * f + x], (8, 128)), pltpu.roll(c, 1, 0))
            down = jnp.where(sub == 7, jnp.broadcast_to(blk_high[2 * f + x], (8, 128)), pltpu.roll(c, 7, 0))
            left = jnp.where(lane == 0, 0.0, pltpu.roll(c, 1, 1))
            right = jnp.where(lane == 127, 0.0, pltpu.roll(c, 127, 1))
            row.append(((high + low) + (down + up) + (right + left)) - 6.0 * c)
        out.append(row)
    return out


def tendency(cells, beside, diffusivity, coupling):
    count = len(cells)
    out = []
    for f in range(count):
        row = []
        for x in range(2):
            total = coupling[f, 0] * cells[0][x]
            for g in range(1, count):
                total = total + coupling[f, g] * cells[g][x]
            row.append(diffusivity[f] * beside[f][x] + total)
        out.append(row)
    return out


def split3(x):
    high = x.astype(BF16)
    rest = x - high.astype(F32)
    mid = rest.astype(BF16)
    low = (rest - mid.astype(F32)).astype(BF16)
    return high, mid, low


def dot_rows(a, b):
    return lax.dot_general(a, b, (((1,), (1,)), ((), ())), preferred_element_type=F32)


def dot_columns(a, b):
    return lax.dot_general(a, b, (((0,), (0,)), ((), ())), preferred_element_type=F32)


def gather_kernel(
    edges,
    hist_ref, fields_ref, levels_ref, diff_ref, coup_ref,
    gram_ref, snap_out, fine_out,
    hist, wide, snap, fine,
    edge_sect, edge_blk, stage_blk, stage_sect,
    h_send, h_half, h_slots, h_part, h_final,
    f_send, f_half, f_slots, f_part, f_final,
    local_sem, send_sem, recv_sem,
):
    n_sect, n_blk = edges
    sect = lax.axis_index("sect")
    blk = lax.axis_index("blk")
    x, y, z, core = position()
    other = device(x, y, z, 1 - core)
    along_x = [device((x + k) % RING, y, z, core) for k in range(1, RING)]
    along_y = [device(x, (y + k) % RING, z, core) for k in range(1, RING)]
    along_z = [device(x, y, (z + k) % RING, core) for k in range(1, RING)]
    sect_down = ((sect + n_sect - 1) % n_sect, blk)
    sect_up = ((sect + 1) % n_sect, blk)
    blk_down = (sect, (blk + n_blk - 1) % n_blk)
    blk_up = (sect, (blk + 1) % n_blk)
    peers = [other] + along_x + along_y + along_z + [sect_down, sect_up, blk_down, blk_up]

    load = pltpu.make_async_copy(hist_ref, hist, local_sem.at[0])
    load.start()
    barrier = pltpu.get_barrier_semaphore()
    for peer in peers:
        pl.semaphore_signal(barrier, inc=1, device_id=peer, device_id_type=MESH)

    def send(src, dst, index, target):
        pltpu.make_async_remote_copy(
            src_ref=src, dst_ref=dst, send_sem=send_sem.at[index], recv_sem=recv_sem.at[index],
            device_id=target, device_id_type=MESH,
        ).start()

    def wait_recv(ref, index):
        pltpu.make_async_copy(ref, ref, recv_sem.at[index]).wait()

    def wait_send(ref, index):
        pltpu.make_async_copy(ref, ref, send_sem.at[index]).wait()

    sub = lax.broadcasted_iota(jnp.int32, (8, 128), 0)
    lane = lax.broadcasted_iota(jnp.int32, (8, 128), 1)
    count = fields_ref.shape[0]
    stored = hist_ref.shape[0]
    columns = stored + 2 * count
    half_columns = columns // 2

    load.wait()
    wide[0:stored * 16, :] = hist[...].astype(F32).reshape(stored * 16, 128)
    wide[stored * 16:, :] = jnp.zeros((2 * count * 16, 128), F32)
    for q in range(16):
        snap[:, 128 * q:128 * q + 128] = wide[pl.ds(q, columns, stride=16), :].astype(BF16)
    gram = dot_rows(snap[...], snap[...])
    i = lax.broadcasted_iota(jnp.int32, (128, 128), 0)
    j = lax.broadcasted_iota(jnp.int32, (128, 128), 1)
    corner = gram[128:, 128:]
    diagonal = jnp.sum(jnp.where(i == j, corner, 0.0), axis=0, keepdims=True)
    folded = jnp.where(i <= j, gram[:128, :128], corner)
    folded = jnp.where((i == 127) & (j < 112), diagonal, folded)
    h_send[0] = folded.reshape(RING, 16, 128)
    h_send[1] = gram[:128, 128:].reshape(RING, 16, 128)

    cells = [[fields_ref[f, k] for k in range(2)] for f in range(count)]

    def send_edges(values, first):
        for f in range(count):
            for k in range(2):
                if first == 1:
                    stage_sect[k, f] = values[f][k]
                stage_blk[first, 0, 2 * f + k:2 * f + k + 1, :] = values[f][k][0:1, :]
                stage_blk[first, 1, 2 * f + k:2 * f + k + 1, :] = values[f][k][7:8, :]
        low = fields_ref.at[:, 0] if first == 0 else stage_sect.at[0]
        high = fields_ref.at[:, 1] if first == 0 else stage_sect.at[1]
        send(low, edge_sect.at[first, 1], 2 * first, sect_down)
        send(high, edge_sect.at[first, 0], 2 * first, sect_up)
        send(stage_blk.at[first, 0], edge_blk.at[first, 1], 2 * first + 1, blk_down)
        send(stage_blk.at[first, 1], edge_blk.at[first, 0], 2 * first + 1, blk_up)

    def take_edges(first):
        wait_recv(edge_sect.at[first], 2 * first)
        wait_recv(edge_blk.at[first], 2 * first + 1)
        sect_low = [jnp.where(sect == 0, 0.0, edge_sect[first, 0, f]) for f in range(count)]
        sect_high = [jnp.where(sect == n_sect - 1, 0.0, edge_sect[first, 1, f]) for f in range(count)]
        blk_low = [jnp.where(blk == 0, 0.0, edge_blk[first, 0, r:r + 1, :]) for r in range(2 * count)]
        blk_high = [jnp.where(blk == n_blk - 1, 0.0, edge_blk[first, 1, r:r + 1, :]) for r in range(2 * count)]
        return sect_low, sect_high, blk_low, blk_high

    pl.semaphore_wait(barrier, len(peers))
    send_edges(cells, 0)
    send(h_send.at[1 - core], h_half.at[0], 4, other)

    refined = jnp.zeros((8, 128), jnp.int32) + levels_ref[0, 0]
    refined = refined.astype(F32)
    stride = 1.0 / (1.0 + refined)

    wait_recv(h_half.at[0], 4)
    h_half[1] = h_send[core] + h_half[0]
    for k in range(1, RING):
        send(h_half.at[1, (y + k) % RING], h_slots.at[0, k - 1], 5, along_y[k - 1])

    beside = neighbour_sum(cells, *take_edges(0), sub, lane)
    tend = tendency(cells, beside, diff_ref, coup_ref)
    first_state = [[cells[f][k] + stride * tend[f][k] for k in range(2)] for f in range(count)]
    send_edges(first_state, 1)

    wait_recv(h_slots.at[0], 5)
    total = h_half[1, y]
    for k in range(RING - 1):
        total = total + h_slots[0, k]
    h_part[0] = total
    for k in range(1, RING):
        send(h_part.at[0], h_slots.at[1, k - 1], 6, along_x[k - 1])

    beside = neighbour_sum(first_state, *take_edges(1), sub, lane)
    tend = tendency(first_state, beside, diff_ref, coup_ref)
    weight = refined * stride
    for f in range(count):
        for k in range(2):
            final = first_state[f][k] + weight * tend[f][k]
            row = (stored + f) * 16 + 8 * k
            wide[row:row + 8, :] = final
            row = (stored + count + f) * 16 + 8 * k
            wide[row:row + 8, :] = final - cells[f][k]
    for q in range(16):
        high, mid, low = split3(wide[pl.ds((columns - 16) * 16 + q, 16, stride=16), :])
        snap[columns - 16:columns, 128 * q:128 * q + 128] = high
        fine[0, :, 128 * q:128 * q + 128] = mid
        fine[1, :, 128 * q:128 * q + 128] = low
    keep_snap = pltpu.make_async_copy(snap, snap_out, local_sem.at[1])
    keep_snap.start()
    keep_fine = pltpu.make_async_copy(fine, fine_out, local_sem.at[2])
    keep_fine.start()
    pieces = jnp.concatenate([snap[columns - 16:columns, :], fine[0], fine[1]], axis=0)
    fresh = dot_rows(pieces, snap[...])
    fresh_fine = dot_rows(pieces, pieces[16:])
    fresh = fresh[0:16] + fresh[16:32] + fresh[32:48]
    extra = fresh_fine[0:16, 0:16] + (fresh_fine[0:16, 16:32] + fresh_fine[16:32, 0:16])
    f_send[0] = fresh[:, :half_columns]
    f_send[1] = fresh[:, half_columns:]
    f_send[1, :, half_columns - 16:] = fresh[:, columns - 16:] + extra
    send(f_send.at[1 - core], f_half.at[0], 7, other)

    wait_recv(f_half.at[0], 7)
    f_part[0] = f_send[core] + f_half[0]
    for k in range(1, RING):
        send(f_part.at[0], f_slots.at[0, k - 1], 8, along_x[k - 1])

    wait_recv(h_slots.at[1], 6)
    total = h_part[0]
    for k in range(RING - 1):
        total = total + h_slots[1, k]
    h_part[1] = total
    for k in range(1, RING):
        send(h_part.at[1], h_slots.at[2, k - 1], 9, along_z[k - 1])

    wait_recv(f_slots.at[0], 8)
    total = f_part[0]
    for k in range(RING - 1):
        total = total + f_slots[0, k]
    f_part[1] = total
    for k in range(1, RING):
        send(f_part.at[1], f_slots.at[1, k - 1], 10, along_z[k - 1])

    wait_recv(h_slots.at[2], 9)
    total = h_part[1]
    for k in range(RING - 1):
        total = total + h_slots[2, k]
    h_final[core, y] = total
    for k in range(1, RING):
        send(h_final.at[core, y], h_final.at[core, y], 11, along_y[k - 1])

    wait_recv(f_slots.at[1], 10)
    total = f_part[1]
    for k in range(RING - 1):
        total = total + f_slots[1, k]
    f_part[2] = total
    for k in range(1, RING):
        send(f_part.at[2], f_slots.at[2, k - 1], 12, along_y[k - 1])

    wait_recv(h_slots.at[2], 11)
    send(h_final.at[core], h_final.at[core], 13, other)

    wait_recv(f_slots.at[2], 12)
    total = f_part[2]
    for k in range(RING - 1):
        total = total + f_slots[2, k]
    f_final[core] = total
    send(f_final.at[core], f_final.at[core], 14, other)

    wait_recv(h_final.at[0], 13)
    wait_recv(f_final.at[0], 14)

    folded = h_final[0].reshape(128, 128)
    turned = folded.T
    first = jnp.where(i <= j, folded, turned)
    corner = jnp.where(i > j, folded, turned)
    corner = jnp.where(i == j, jnp.broadcast_to(folded[127:128, :], (128, 128)), corner)
    side = h_final[1].reshape(128, 128)
    low_rows = jnp.concatenate([jnp.zeros((112, 128), F32), f_final[0]], axis=0).T
    high_rows = jnp.concatenate([jnp.zeros((112, 128), F32), f_final[1]], axis=0)
    corner = jnp.where(i >= 112, high_rows, jnp.where(j >= 112, high_rows.T, corner))
    side = jnp.where(j >= 112, low_rows, side)
    gram_ref[0:128, 0:128] = first
    gram_ref[0:128, 128:] = side
    gram_ref[128:, 0:128] = side.T
    gram_ref[128:, 128:] = corner

    for first_round in range(2):
        wait_send(edge_sect.at[first_round], 2 * first_round)
        wait_send(edge_blk.at[first_round], 2 * first_round + 1)
    wait_send(h_half.at[0], 4)
    wait_send(h_slots.at[0], 5)
    wait_send(h_slots.at[0], 6)
    wait_send(f_half.at[0], 7)
    wait_send(f_slots.at[0], 8)
    wait_send(h_slots.at[0], 9)
    wait_send(f_slots.at[0], 10)
    wait_send(h_slots.at[0], 11)
    wait_send(f_slots.at[0], 12)
    wait_send(h_final.at[0], 13)
    wait_send(f_final.at[0], 14)
    keep_snap.wait()
    keep_fine.wait()


def eliminate(rows, col0, width):
    count = BLOCK // 8
    tiles = width // 128
    values = [rows[8 * v:8 * v + 8] for v in range(count)]
    pivots = [jnp.zeros((8, 128), F32) for _ in range(count)]
    sub = lax.broadcasted_iota(jnp.int32, (8, 128), 0)
    for start in range(0, BLOCK, GROUP):
        v0 = start // 8
        spread = [
            [jnp.broadcast_to(values[v][:, col0 + start + p:col0 + start + p + 1], (8, 128)) for v in range(v0, count)]
            for p in range(GROUP)
        ]
        for p in range(GROUP):
            vp, s = (start + p) // 8, (start + p) % 8
            raw = spread[p]
            pivot = jnp.broadcast_to(raw[vp - v0][s:s + 1, :], (8, 128))
            inverse = 1.0 / pivot
            pivots[vp] = jnp.where(sub == s, pivot, pivots[vp])
            factors = {}
            for v in range(vp, count):
                factor = raw[v - v0] * inverse
                factors[v] = jnp.where(sub > s, factor, 0.0) if v == vp else factor
            for later in range(p + 1, GROUP):
                vl, sl = (start + later) // 8, (start + later) % 8
                across = jnp.broadcast_to(raw[vl - v0][sl:sl + 1, :], (8, 128))
                for v in range(vp, count):
                    spread[later][v - v0] = spread[later][v - v0] - factors[v] * across
            row = jnp.broadcast_to(values[vp][s:s + 1, :], (8, width))
            for v in range(vp, count):
                if v == vp and s == 7:
                    continue
                values[v] = values[v] - jnp.concatenate([factors[v]] * tiles, axis=1) * row
    return jnp.concatenate(
        [values[v] * jnp.concatenate([lax.rsqrt(pivots[v])] * tiles, axis=1) for v in range(count)], axis=0
    )


def finish_kernel(
    total_rows,
    gram_ref, snap_ref, fine_ref,
    modes_ref, factor_ref,
    work, inverse, snap, fine, modes, local_sem,
):
    size = gram_ref.shape[0]
    load_snap = pltpu.make_async_copy(snap_ref, snap, local_sem.at[0])
    load_snap.start()
    load_fine = pltpu.make_async_copy(fine_ref, fine, local_sem.at[1])
    load_fine.start()
    scale = math.sqrt(total_rows)
    shape = (size, size)
    identity = lax.broadcasted_iota(jnp.int32, shape, 0) == lax.broadcasted_iota(jnp.int32, shape, 1)
    work[:, :size] = gram_ref[...]
    work[:, size:] = identity.astype(F32)
    rows = work[0:BLOCK, :]
    for b0 in range(0, size, BLOCK):
        done = eliminate(rows, b0, 2 * size)
        i = lax.broadcasted_iota(jnp.int32, (BLOCK, size), 0) + b0
        j = lax.broadcasted_iota(jnp.int32, (BLOCK, size), 1)
        upper = jnp.where(j >= i, done[:, :size], 0.0)
        factor_ref[b0:b0 + BLOCK, :] = upper * (1.0 / scale)
        inverse[b0:b0 + BLOCK, :] = done[:, size:] * scale
        b1 = b0 + BLOCK
        if b1 < size:
            h, m, l = split3(upper)
            left = jnp.concatenate([h, h, m, m, h, l], axis=0)
            h, m, l = split3(done)
            right = jnp.concatenate([h, m, h, m, l, h], axis=0)
            rows = work[b1:b1 + BLOCK, :] - dot_columns(left[:, b1:b1 + BLOCK], right)
            if b1 + BLOCK < size:
                work[b1 + BLOCK:, :] = work[b1 + BLOCK:, :] - dot_columns(left[:, b1 + BLOCK:], right)
    load_snap.wait()
    load_fine.wait()
    step = 64
    stores = []
    tail = jnp.concatenate([fine[0], fine[0], fine[0], fine[1]], axis=0)
    for r0 in range(0, size, step):
        h, m, l = split3(inverse[r0:r0 + step, :])
        out = jnp.dot(h, snap[...], preferred_element_type=F32)
        out = out + jnp.dot(m, snap[...], preferred_element_type=F32)
        out = out + jnp.dot(l, snap[...], preferred_element_type=F32)
        last = jnp.concatenate([h[:, size - 16:], m[:, size - 16:], l[:, size - 16:], h[:, size - 16:]], axis=1)
        out = out + jnp.dot(last, tail, preferred_element_type=F32)
        for q in range(16):
            modes[pl.ds(r0 * 16 + q, step, stride=16), :] = out[:, 128 * q:128 * q + 128]
        store = pltpu.make_async_copy(
            modes.at[pl.ds(r0 * 16, step * 16)], modes_ref.at[pl.ds(r0 * 16, step * 16)], local_sem.at[2 + r0 // step]
        )
        store.start()
        stores.append(store)
    for store in stores:
        store.wait()


def shards(fields, history, levels, diffusivity, coupling):
    edges = (lax.axis_size("sect"), lax.axis_size("blk"))
    stored, count_x, count_y, count_z = history.shape
    count = fields.shape[0]
    columns = stored + 2 * count
    local = count_x * count_y * count_z
    vmem = pl.BlockSpec(memory_space=pltpu.VMEM)
    smem = pl.BlockSpec(memory_space=pltpu.SMEM)
    anywhere = pl.BlockSpec(memory_space=pl.ANY)
    gram, snap, fine = pl.pallas_call(
        functools.partial(gather_kernel, edges),
        out_shape=[
            jax.ShapeDtypeStruct((columns, columns), F32),
            jax.ShapeDtypeStruct((columns, local), BF16),
            jax.ShapeDtypeStruct((2, 16, local), BF16),
        ],
        in_specs=[anywhere, vmem, smem, smem, smem],
        out_specs=[vmem, anywhere, anywhere],
        scratch_shapes=[
            pltpu.VMEM(history.shape, BF16),
            pltpu.VMEM((columns * 16, 128), F32),
            pltpu.VMEM((columns, local), BF16),
            pltpu.VMEM((2, 16, local), BF16),
            pltpu.VMEM((2, 2, count, 8, 128), F32),
            pltpu.VMEM((2, 2, 16, 128), F32),
            pltpu.VMEM((2, 2, 16, 128), F32),
            pltpu.VMEM((2, count, 8, 128), F32),
            pltpu.VMEM((2, RING, 16, 128), F32),
            pltpu.VMEM((2, RING, 16, 128), F32),
            pltpu.VMEM((3, RING - 1, 16, 128), F32),
            pltpu.VMEM((2, 16, 128), F32),
            pltpu.VMEM((2, RING, 16, 128), F32),
            pltpu.VMEM((2, 16, 128), F32),
            pltpu.VMEM((1, 16, 128), F32),
            pltpu.VMEM((3, RING - 1, 16, 128), F32),
            pltpu.VMEM((3, 16, 128), F32),
            pltpu.VMEM((2, 16, 128), F32),
            pltpu.SemaphoreType.DMA((3,)),
            pltpu.SemaphoreType.DMA((15,)),
            pltpu.SemaphoreType.DMA((15,)),
        ],
        compiler_params=pltpu.CompilerParams(
            collective_id=0, has_side_effects=True, vmem_limit_bytes=32 << 20
        ),
        name="gather",
    )(history, fields, levels, diffusivity, coupling)
    modes, factor = pl.pallas_call(
        functools.partial(finish_kernel, local * edges[0] * edges[1]),
        out_shape=[
            jax.ShapeDtypeStruct((columns * 16, 128), F32),
            jax.ShapeDtypeStruct((columns, columns), F32),
        ],
        in_specs=[vmem, anywhere, anywhere],
        out_specs=[anywhere, vmem],
        scratch_shapes=[
            pltpu.VMEM((columns, 2 * columns), F32),
            pltpu.VMEM((columns, columns), F32),
            pltpu.VMEM((columns, local), BF16),
            pltpu.VMEM((2, 16, local), BF16),
            pltpu.VMEM((columns * 16, 128), F32),
            pltpu.SemaphoreType.DMA((6,)),
        ],
        compiler_params=pltpu.CompilerParams(vmem_limit_bytes=32 << 20),
        name="finish",
    )(gram, snap, fine)
    return modes.reshape(columns, count_x, count_y, count_z), factor


def solution(mesh):
    return jax.shard_map(
        shards,
        mesh=mesh,
        in_specs=(
            P(None, "sect", "blk", None),
            P(None, "sect", "blk", None),
            P("sect", "blk"),
            P(),
            P(),
        ),
        out_specs=(P(None, "sect", "blk", None), P()),
        check_vma=False,
    )
```

```python
import functools
import math

import jax
import jax.numpy as jnp
from jax import lax
from jax.experimental import pallas as pl
from jax.experimental.pallas import tpu as pltpu
from jax.sharding import PartitionSpec as P

F32 = jnp.float32
BF16 = jnp.bfloat16
MESH = pl.DeviceIdType.MESH
Z_CHIPS = 8
Y_CHIPS = 8
X_LOW = 4
RING = 8
BLOCK = 32
GROUP = 16
HALF = 128
TAIL = 16


def position():
    sect = lax.axis_index("sect")
    blk = lax.axis_index("blk")
    x = (sect // Z_CHIPS) * X_LOW + blk // (2 * Y_CHIPS)
    y = (blk // 2) % Y_CHIPS
    return x, y, sect % Z_CHIPS, blk % 2


def device(x, y, z, core):
    return ((x // X_LOW) * Z_CHIPS + z, ((x % X_LOW) * Y_CHIPS + y) * 2 + core)


def neighbour_sum(cells, sect_low, sect_high, blk_low, blk_high, sub, lane):
    out = []
    for f in range(len(cells)):
        row = []
        for x in range(2):
            c = cells[f][x]
            low = sect_low[f] if x == 0 else cells[f][0]
            high = sect_high[f] if x == 1 else cells[f][1]
            up = jnp.where(sub == 0, jnp.broadcast_to(blk_low[2 * f + x], (8, 128)), pltpu.roll(c, 1, 0))
            down = jnp.where(sub == 7, jnp.broadcast_to(blk_high[2 * f + x], (8, 128)), pltpu.roll(c, 7, 0))
            left = jnp.where(lane == 0, 0.0, pltpu.roll(c, 1, 1))
            right = jnp.where(lane == 127, 0.0, pltpu.roll(c, 127, 1))
            row.append(((high + low) + (down + up) + (right + left)) - 6.0 * c)
        out.append(row)
    return out


def tendency(cells, beside, diffusivity, coupling):
    count = len(cells)
    out = []
    for f in range(count):
        row = []
        for x in range(2):
            total = coupling[f, 0] * cells[0][x]
            for g in range(1, count):
                total = total + coupling[f, g] * cells[g][x]
            row.append(diffusivity[f] * beside[f][x] + total)
        out.append(row)
    return out


def split3(x):
    high = x.astype(BF16)
    rest = x - high.astype(F32)
    mid = rest.astype(BF16)
    low = (rest - mid.astype(F32)).astype(BF16)
    return high, mid, low


def dot_rows(a, b):
    return lax.dot_general(a, b, (((1,), (1,)), ((), ())), preferred_element_type=F32)


def dot_columns(a, b):
    return lax.dot_general(a, b, (((0,), (0,)), ((), ())), preferred_element_type=F32)


def eliminate(rows, col0):
    size, width = rows.shape
    count = size // 8
    tiles = width // 128
    values = [rows[8 * v:8 * v + 8] for v in range(count)]
    pivots = [jnp.zeros((8, 128), F32) for _ in range(count)]
    sub = lax.broadcasted_iota(jnp.int32, (8, 128), 0)
    for start in range(0, size, GROUP):
        v0 = start // 8
        spread = [
            [jnp.broadcast_to(values[v][:, col0 + start + p:col0 + start + p + 1], (8, 128)) for v in range(v0, count)]
            for p in range(GROUP)
        ]
        for p in range(GROUP):
            vp, s = (start + p) // 8, (start + p) % 8
            raw = spread[p]
            pivot = jnp.broadcast_to(raw[vp - v0][s:s + 1, :], (8, 128))
            inverse = 1.0 / pivot
            pivots[vp] = jnp.where(sub == s, pivot, pivots[vp])
            factors = {}
            for v in range(vp, count):
                factor = raw[v - v0] * inverse
                factors[v] = jnp.where(sub > s, factor, 0.0) if v == vp else factor
            for later in range(p + 1, GROUP):
                vl, sl = (start + later) // 8, (start + later) % 8
                across = jnp.broadcast_to(raw[vl - v0][sl:sl + 1, :], (8, 128))
                for v in range(vp, count):
                    spread[later][v - v0] = spread[later][v - v0] - factors[v] * across
            row = jnp.broadcast_to(values[vp][s:s + 1, :], (8, width))
            for v in range(vp, count):
                if v == vp and s == 7:
                    continue
                values[v] = values[v] - jnp.concatenate([factors[v]] * tiles, axis=1) * row
    return jnp.concatenate(
        [values[v] * jnp.concatenate([lax.rsqrt(pivots[v])] * tiles, axis=1) for v in range(count)], axis=0
    )


def pack_left(x, axis):
    h, m, l = split3(x)
    return jnp.concatenate([h, h, m, m, h, l], axis=axis)


def pack_right(x, axis):
    h, m, l = split3(x)
    return jnp.concatenate([h, m, h, m, l, h], axis=axis)


def eliminate_half(work, ends, store, between):
    b0 = 0
    rows = work[0:ends[0], :]
    for index, b1 in enumerate(ends):
        done = eliminate(rows, b0)
        i = lax.broadcasted_iota(jnp.int32, (b1 - b0, HALF), 0) + b0
        j = lax.broadcasted_iota(jnp.int32, (b1 - b0, HALF), 1)
        upper = jnp.where(j >= i, done[:, :HALF], 0.0)
        store(b0, b1, upper, done[:, HALF:])
        if index + 1 < len(ends):
            b2 = ends[index + 1]
            left = pack_left(upper, 0)
            right = pack_right(done, 0)
            rows = work[b1:b2, :] - dot_columns(left[:, b1:b2], right)
            if index + 2 < len(ends):
                b3 = ends[-1]
                work[b2:b3, :] = work[b2:b3, :] - dot_columns(left[:, b2:b3], right)
        between(index)
        b0 = b1


def gather_kernel(
    edges, total_rows,
    hist_ref, fields_ref, levels_ref, diff_ref, coup_ref,
    inverse_ref, upper_ref, snap, fine,
    hist, wide, fields, diff, coup,
    edge_sect, edge_blk, stage_blk, stage_sect,
    p_send, p_half, p_slots, p_part, p_final,
    h_send, h_half, h_slots, h_part, h_final,
    f_send, f_half, f_slots, f_part, f_final,
    work, work2,
    local_sem, send_sem, recv_sem,
):
    n_sect, n_blk = edges
    sect = lax.axis_index("sect")
    blk = lax.axis_index("blk")
    x, y, z, core = position()
    other = device(x, y, z, 1 - core)
    along_x = [device((x + k) % RING, y, z, core) for k in range(1, RING)]
    along_y = [device(x, (y + k) % RING, z, core) for k in range(1, RING)]
    along_z = [device(x, y, (z + k) % RING, core) for k in range(1, RING)]
    along = [along_x, along_y, along_z]
    sect_down = ((sect + n_sect - 1) % n_sect, blk)
    sect_up = ((sect + 1) % n_sect, blk)
    blk_down = (sect, (blk + n_blk - 1) % n_blk)
    blk_up = (sect, (blk + 1) % n_blk)
    peers = [other] + along_x + along_y + along_z + [sect_down, sect_up, blk_down, blk_up]

    count = fields_ref.shape[0]
    stored = hist_ref.shape[0]
    columns = stored + 2 * count
    scale = math.sqrt(total_rows)

    loads = [
        pltpu.make_async_copy(hist_ref.at[0:HALF], hist.at[0:HALF], local_sem.at[0]),
        pltpu.make_async_copy(fields_ref, fields, local_sem.at[1]),
        pltpu.make_async_copy(hist_ref.at[HALF:stored], hist.at[HALF:stored], local_sem.at[2]),
        pltpu.make_async_copy(diff_ref, diff, local_sem.at[3]),
        pltpu.make_async_copy(coup_ref, coup, local_sem.at[4]),
    ]
    for load in loads:
        load.start()
    barrier = pltpu.get_barrier_semaphore()
    for peer in peers:
        pl.semaphore_signal(barrier, inc=1, device_id=peer, device_id_type=MESH)

    def send(src, dst, index, target):
        pltpu.make_async_remote_copy(
            src_ref=src, dst_ref=dst, send_sem=send_sem.at[index], recv_sem=recv_sem.at[index],
            device_id=target, device_id_type=MESH,
        ).start()

    def wait_recv(ref, index):
        pltpu.make_async_copy(ref, ref, recv_sem.at[index]).wait()

    def wait_send(ref, index):
        pltpu.make_async_copy(ref, ref, send_sem.at[index]).wait()

    sub = lax.broadcasted_iota(jnp.int32, (8, 128), 0)
    lane = lax.broadcasted_iota(jnp.int32, (8, 128), 1)

    wide[stored * 16:, :] = jnp.zeros((2 * count * 16, 128), F32)
    loads[1].wait()
    cells = [[fields[f, k] for k in range(2)] for f in range(count)]

    def send_edges(values, first):
        for f in range(count):
            for k in range(2):
                stage_sect[first, k, f] = values[f][k]
                stage_blk[first, 0, 2 * f + k:2 * f + k + 1, :] = values[f][k][0:1, :]
                stage_blk[first, 1, 2 * f + k:2 * f + k + 1, :] = values[f][k][7:8, :]
        send(stage_sect.at[first, 0], edge_sect.at[first, 1], 2 * first, sect_down)
        send(stage_sect.at[first, 1], edge_sect.at[first, 0], 2 * first, sect_up)
        send(stage_blk.at[first, 0], edge_blk.at[first, 1], 2 * first + 1, blk_down)
        send(stage_blk.at[first, 1], edge_blk.at[first, 0], 2 * first + 1, blk_up)

    def take_edges(first):
        wait_recv(edge_sect.at[first], 2 * first)
        wait_recv(edge_blk.at[first], 2 * first + 1)
        sect_low = [jnp.where(sect == 0, 0.0, edge_sect[first, 0, f]) for f in range(count)]
        sect_high = [jnp.where(sect == n_sect - 1, 0.0, edge_sect[first, 1, f]) for f in range(count)]
        blk_low = [jnp.where(blk == 0, 0.0, edge_blk[first, 0, r:r + 1, :]) for r in range(2 * count)]
        blk_high = [jnp.where(blk == n_blk - 1, 0.0, edge_blk[first, 1, r:r + 1, :]) for r in range(2 * count)]
        return sect_low, sect_high, blk_low, blk_high

    pl.semaphore_wait(barrier, len(peers))
    send_edges(cells, 0)

    def arrange(low, high, full):
        wide[low * 16:high * 16, :] = hist[low:high].astype(F32).reshape((high - low) * 16, 128)
        for q in range(16):
            snap[low:full, 128 * q:128 * q + 128] = wide[pl.ds(low * 16 + q, full - low, stride=16), :].astype(BF16)

    loads[0].wait()
    arrange(0, HALF, HALF)
    first = snap[0:HALF, :]
    square = dot_rows(first, first)
    third = HALF // 8
    for part in range(3):
        p_send[0, part] = square[third * part:third * part + third, :]
    p_send[1, 0] = square[3 * third:4 * third, :]
    corner = jnp.concatenate([square[64:96, 64:], square[96:128, 64:]], axis=1)
    p_send[1, 1] = corner[0:16]
    p_send[1, 2] = corner[16:32]
    send(p_send.at[1 - core], p_half, 4, other)

    loads[2].wait()
    arrange(HALF, stored, columns)
    second = snap[HALF:columns, :]
    h_send[0] = dot_rows(first, second).reshape(RING, 16, 128)
    h_send[1] = dot_rows(second, second).reshape(RING, 16, 128)
    send(h_send.at[1 - core], h_half.at[0], 5, other)

    def p_phase(phase):
        for k in range(RING - 1):
            for part in range(3):
                send(p_part.at[phase, part], p_slots.at[phase, part, k], 6 + phase, along[(part + phase) % 3][k])

    def p_sum(phase):
        wait_recv(p_slots.at[phase], 6 + phase)
        total = p_part[phase]
        for k in range(RING - 1):
            total = total + p_slots[phase, :, k]
        return total

    def total_of(own, slots):
        for k in range(RING - 1):
            own = own + slots[k]
        return own

    wait_recv(p_half, 4)
    p_part[0] = p_send[core] + p_half[...]
    p_phase(0)

    wait_recv(h_half.at[0], 5)
    h_half[1] = h_send[core] + h_half[0]
    for k in range(1, RING):
        send(h_half.at[1, (y + k) % RING], h_slots.at[0, k - 1], 9, along_y[k - 1])

    for load in loads[3:]:
        load.wait()
    refined = (jnp.zeros((8, 128), jnp.int32) + levels_ref[0, 0]).astype(F32)
    stride = 1.0 / (1.0 + refined)
    diffusivity = [jnp.broadcast_to(diff[0:1, f:f + 1], (8, 128)) for f in range(count)]
    coupling = {
        (f, g): jnp.broadcast_to(coup[f:f + 1, g:g + 1], (8, 128)) for f in range(count) for g in range(count)
    }
    beside = neighbour_sum(cells, *take_edges(0), sub, lane)
    tend = tendency(cells, beside, diffusivity, coupling)
    first_state = [[cells[f][k] + stride * tend[f][k] for k in range(2)] for f in range(count)]
    send_edges(first_state, 1)

    p_part[1] = p_sum(0)
    p_phase(1)

    wait_recv(h_slots.at[0], 9)
    h_part[0] = total_of(h_half[1, y], h_slots[0])
    for k in range(1, RING):
        send(h_part.at[0], h_slots.at[1, k - 1], 10, along_x[k - 1])

    p_part[2] = p_sum(1)
    p_phase(2)

    wait_recv(h_slots.at[1], 10)
    h_part[1] = total_of(h_part[0], h_slots[1])
    for k in range(1, RING):
        send(h_part.at[1], h_slots.at[2, k - 1], 11, along_z[k - 1])

    beside = neighbour_sum(first_state, *take_edges(1), sub, lane)
    tend = tendency(first_state, beside, diffusivity, coupling)
    weight = refined * stride
    for f in range(count):
        for k in range(2):
            final = first_state[f][k] + weight * tend[f][k]
            row = (stored + f) * 16 + 8 * k
            wide[row:row + 8, :] = final
            row = (stored + count + f) * 16 + 8 * k
            wide[row:row + 8, :] = final - cells[f][k]
    for q in range(16):
        high, mid, low = split3(wide[pl.ds((columns - TAIL) * 16 + q, TAIL, stride=16), :])
        snap[columns - TAIL:columns, 128 * q:128 * q + 128] = high
        fine[0, :, 128 * q:128 * q + 128] = mid
        fine[1, :, 128 * q:128 * q + 128] = low
    pieces = jnp.concatenate([snap[columns - TAIL:columns, :], fine[0], fine[1]], axis=0)
    fresh = dot_rows(pieces, snap[...])
    fresh_fine = dot_rows(pieces, pieces[TAIL:])
    fresh = fresh[0:TAIL] + fresh[TAIL:2 * TAIL] + fresh[2 * TAIL:]
    extra = fresh_fine[0:TAIL, 0:TAIL] + (fresh_fine[0:TAIL, TAIL:] + fresh_fine[TAIL:2 * TAIL, 0:TAIL])
    f_send[0] = fresh[:, :HALF]
    f_send[1] = fresh[:, HALF:]
    f_send[1, :, HALF - TAIL:] = fresh[:, columns - TAIL:] + extra
    send(f_send.at[1 - core], f_half.at[0], 12, other)

    wait_recv(f_half.at[0], 12)
    f_part[0] = f_send[core] + f_half[0]
    for k in range(1, RING):
        send(f_part.at[0], f_slots.at[0, k - 1], 13, along_x[k - 1])

    p_final[core] = p_sum(2)
    send(p_final.at[core], p_final.at[core], 14, other)

    wait_recv(h_slots.at[2], 11)
    h_final[core, y] = total_of(h_part[1], h_slots[2])
    for k in range(1, RING):
        send(h_final.at[core, y], h_final.at[core, y], 15, along_y[k - 1])

    wait_recv(p_final.at[0], 14)

    i = lax.broadcasted_iota(jnp.int32, (HALF, HALF), 0)
    j = lax.broadcasted_iota(jnp.int32, (HALF, HALF), 1)
    identity = (i == j).astype(F32)
    for part in range(3):
        work[16 * part:16 * part + 16, 0:HALF] = p_final[0, part]
    work[48:64, 0:HALF] = p_final[1, 0]
    lower = jnp.concatenate([p_final[1, 1], p_final[1, 2]], axis=0)
    work[64:96, 0:HALF] = jnp.concatenate([jnp.zeros((32, 64), F32), lower[:, :64]], axis=1)
    work[96:128, 0:HALF] = jnp.concatenate([jnp.zeros((32, 64), F32), lower[:, 64:]], axis=1)
    work[:, HALF:] = identity
    inverse_ref[0:HALF, HALF:] = jnp.zeros((HALF, HALF), F32)
    inverse_ref[columns - TAIL:, :] = jnp.zeros((TAIL, columns), F32)
    upper_ref[HALF:, 0:HALF] = jnp.zeros((HALF, HALF), F32)

    def store_first(b0, b1, upper, solved):
        upper_ref[b0:b1, 0:HALF] = upper * (1.0 / scale)
        inverse_ref[b0:b1, 0:HALF] = solved

    def between_first(index):
        if index == 1:
            wait_recv(f_slots.at[0], 13)
            f_part[1] = total_of(f_part[0], f_slots[0])
            for k in range(1, RING):
                send(f_part.at[1], f_slots.at[1, k - 1], 16, along_z[k - 1])

    eliminate_half(work, [32, 64, 96, 128], store_first, between_first)

    wait_recv(h_slots.at[2], 15)
    send(h_final.at[core], h_final.at[core], 17, other)
    wait_recv(f_slots.at[1], 16)
    f_part[2] = total_of(f_part[1], f_slots[1])
    for k in range(1, RING):
        send(f_part.at[2], f_slots.at[2, k - 1], 18, along_y[k - 1])
    wait_recv(h_final.at[0], 17)

    solved = inverse_ref[0:HALF, 0:HALF]
    side = jnp.dot(
        pack_left(solved, 1), pack_right(h_final[0].reshape(HALF, HALF), 0), preferred_element_type=F32
    )
    product = dot_columns(pack_left(side, 0), pack_right(jnp.concatenate([side, solved], axis=1), 0))
    work2[:, 0:HALF] = h_final[1].reshape(HALF, HALF) - product[:, :HALF]
    work2[:, HALF:2 * HALF] = -product[:, HALF:]
    work2[:, 2 * HALF:] = identity
    upper_ref[0:HALF, HALF:] = side * (1.0 / scale)

    def store_second(b0, b1, upper, solved):
        upper_ref[HALF + b0:HALF + b1, HALF:] = upper * (1.0 / scale)
        inverse_ref[HALF + b0:HALF + b1, :] = solved

    def between_second(index):
        if index == 2:
            wait_recv(f_slots.at[2], 18)
            f_final[core] = total_of(f_part[2], f_slots[2])
            send(f_final.at[core], f_final.at[core], 19, other)

    eliminate_half(work2, [32, 64, 96, HALF - TAIL], store_second, between_second)

    wait_recv(f_final.at[0], 19)
    row = lax.broadcasted_iota(jnp.int32, (TAIL, columns), 0)
    col = lax.broadcasted_iota(jnp.int32, (TAIL, columns), 1)
    last = jnp.concatenate([f_final[0], f_final[1]], axis=1)
    solved = inverse_ref[...]
    below = dot_rows(
        pack_left(jnp.where(col < columns - TAIL, last, 0.0), 1), pack_right(solved, 1)
    )
    left = pack_left(below, 1)
    placed = jnp.concatenate([jnp.zeros((HALF - TAIL, columns), F32), below], axis=0)
    rest = last[:, HALF:] - dot_rows(left, pack_right(placed, 1))
    onward = (col == row + (columns - TAIL)).astype(F32) - jnp.dot(
        left, pack_right(solved, 0), preferred_element_type=F32
    )
    done = eliminate(jnp.concatenate([rest, onward], axis=1), HALF - TAIL)
    inverse_ref[columns - TAIL:, :] = done[:, HALF:]
    turned = placed.T
    right_lanes = lax.broadcasted_iota(jnp.int32, (columns - TAIL, HALF), 1) >= HALF - TAIL
    upper_ref[0:columns - TAIL, HALF:] = jnp.where(
        right_lanes, turned[0:columns - TAIL] * (1.0 / scale), upper_ref[0:columns - TAIL, HALF:]
    )
    row = lax.broadcasted_iota(jnp.int32, (TAIL, HALF), 0)
    col = lax.broadcasted_iota(jnp.int32, (TAIL, HALF), 1)
    upper_ref[columns - TAIL:, HALF:] = jnp.where(
        col >= row + (HALF - TAIL), done[:, :HALF] * (1.0 / scale), 0.0
    )

    for round_ in range(2):
        wait_send(edge_sect.at[round_], 2 * round_)
        wait_send(edge_blk.at[round_], 2 * round_ + 1)
    wait_send(p_half, 4)
    wait_send(h_half.at[0], 5)
    for phase in range(3):
        wait_send(p_slots.at[phase], 6 + phase)
        wait_send(h_slots.at[phase], 9 + phase)
    wait_send(f_half.at[0], 12)
    wait_send(f_slots.at[0], 13)
    wait_send(p_final.at[0], 14)
    wait_send(h_slots.at[0], 15)
    wait_send(f_slots.at[1], 16)
    wait_send(h_final.at[0], 17)
    wait_send(f_slots.at[2], 18)
    wait_send(f_final.at[0], 19)


def finish_kernel(
    total_rows,
    inverse_ref, upper_ref, snap, fine,
    modes_ref, factor_ref,
    modes, local_sem,
):
    size = inverse_ref.shape[0]
    scale = math.sqrt(total_rows)
    keep = pltpu.make_async_copy(upper_ref, factor_ref, local_sem.at[0])
    keep.start()
    step = 64
    stores = []
    tail = jnp.concatenate([fine[0], fine[0], fine[0], fine[1]], axis=0)
    for r0 in range(0, size, step):
        h, m, l = split3(inverse_ref[r0:r0 + step, :] * scale)
        out = jnp.dot(h, snap[...], preferred_element_type=F32)
        out = out + jnp.dot(m, snap[...], preferred_element_type=F32)
        out = out + jnp.dot(l, snap[...], preferred_element_type=F32)
        last = jnp.concatenate(
            [h[:, size - TAIL:], m[:, size - TAIL:], l[:, size - TAIL:], h[:, size - TAIL:]], axis=1
        )
        out = out + jnp.dot(last, tail, preferred_element_type=F32)
        for q in range(16):
            modes[pl.ds(r0 * 16 + q, step, stride=16), :] = out[:, 128 * q:128 * q + 128]
        store = pltpu.make_async_copy(
            modes.at[pl.ds(r0 * 16, step * 16)], modes_ref.at[pl.ds(r0 * 16, step * 16)], local_sem.at[1 + r0 // step]
        )
        store.start()
        stores.append(store)
    keep.wait()
    for store in stores:
        store.wait()


def in_hbm(array):
    return pltpu.with_memory_space_constraint(array, pltpu.HBM)


def shards(fields, history, levels, diffusivity, coupling):
    edges = (lax.axis_size("sect"), lax.axis_size("blk"))
    stored, count_x, count_y, count_z = history.shape
    count = fields.shape[0]
    columns = stored + 2 * count
    local = count_x * count_y * count_z
    total_rows = local * edges[0] * edges[1]
    vmem = pl.BlockSpec(memory_space=pltpu.VMEM)
    hbm = pl.BlockSpec(memory_space=pltpu.HBM)
    smem = pl.BlockSpec(memory_space=pltpu.SMEM)
    tile = (16, 128)
    inverse, upper, snap, fine = pl.pallas_call(
        functools.partial(gather_kernel, edges, total_rows),
        out_shape=[
            jax.ShapeDtypeStruct((columns, columns), F32),
            jax.ShapeDtypeStruct((columns, columns), F32),
            jax.ShapeDtypeStruct((columns, local), BF16),
            jax.ShapeDtypeStruct((2, TAIL, local), BF16),
        ],
        in_specs=[hbm, hbm, smem, hbm, hbm],
        out_specs=[vmem, vmem, vmem, vmem],
        scratch_shapes=[
            pltpu.VMEM(history.shape, BF16),
            pltpu.VMEM((columns * 16, 128), F32),
            pltpu.VMEM(fields.shape, F32),
            pltpu.VMEM((1, count), F32),
            pltpu.VMEM((count, count), F32),
            pltpu.VMEM((2, 2, count, 8, 128), F32),
            pltpu.VMEM((2, 2, 16, 128), F32),
            pltpu.VMEM((2, 2, 16, 128), F32),
            pltpu.VMEM((2, 2, count, 8, 128), F32),
            pltpu.VMEM((2, 3) + tile, F32),
            pltpu.VMEM((3,) + tile, F32),
            pltpu.VMEM((3, 3, RING - 1) + tile, F32),
            pltpu.VMEM((3, 3) + tile, F32),
            pltpu.VMEM((2, 3) + tile, F32),
            pltpu.VMEM((2, RING) + tile, F32),
            pltpu.VMEM((2, RING) + tile, F32),
            pltpu.VMEM((3, RING - 1) + tile, F32),
            pltpu.VMEM((2,) + tile, F32),
            pltpu.VMEM((2, RING) + tile, F32),
            pltpu.VMEM((2,) + tile, F32),
            pltpu.VMEM((1,) + tile, F32),
            pltpu.VMEM((3, RING - 1) + tile, F32),
            pltpu.VMEM((3,) + tile, F32),
            pltpu.VMEM((2,) + tile, F32),
            pltpu.VMEM((HALF, 2 * HALF), F32),
            pltpu.VMEM((HALF, 3 * HALF), F32),
            pltpu.SemaphoreType.DMA((5,)),
            pltpu.SemaphoreType.DMA((20,)),
            pltpu.SemaphoreType.DMA((20,)),
        ],
        compiler_params=pltpu.CompilerParams(
            collective_id=0, has_side_effects=True, vmem_limit_bytes=32 << 20
        ),
        name="gather",
    )(in_hbm(history), in_hbm(fields), levels, in_hbm(diffusivity.reshape(1, count)), in_hbm(coupling))
    modes, factor = pl.pallas_call(
        functools.partial(finish_kernel, total_rows),
        out_shape=[
            jax.ShapeDtypeStruct((columns * 16, 128), F32),
            jax.ShapeDtypeStruct((columns, columns), F32),
        ],
        in_specs=[vmem, vmem, vmem, vmem],
        out_specs=[hbm, hbm],
        scratch_shapes=[
            pltpu.VMEM((columns * 16, 128), F32),
            pltpu.SemaphoreType.DMA((5,)),
        ],
        compiler_params=pltpu.CompilerParams(vmem_limit_bytes=32 << 20),
        name="finish",
    )(inverse, upper, snap, fine)
    return modes.reshape(columns, count_x, count_y, count_z), factor


def solution(mesh):
    return jax.shard_map(
        shards,
        mesh=mesh,
        in_specs=(
            P(None, "sect", "blk", None),
            P(None, "sect", "blk", None),
            P("sect", "blk"),
            P(),
            P(),
        ),
        out_specs=(P(None, "sect", "blk", None), P()),
        check_vma=False,
    )
```

```python
import functools
import math

import jax
import jax.numpy as jnp
from jax import lax
from jax.experimental import pallas as pl
from jax.experimental.pallas import tpu as pltpu
from jax.sharding import PartitionSpec as P

F32 = jnp.float32
BF16 = jnp.bfloat16
MESH = pl.DeviceIdType.MESH
Z_CHIPS = 8
Y_CHIPS = 8
X_LOW = 4
RING = 8
BLOCK = 32
GROUP = 16
HALF = 128
TAIL = 16


def position():
    sect = lax.axis_index("sect")
    blk = lax.axis_index("blk")
    x = (sect // Z_CHIPS) * X_LOW + blk // (2 * Y_CHIPS)
    y = (blk // 2) % Y_CHIPS
    return x, y, sect % Z_CHIPS, blk % 2


def device(x, y, z, core):
    return ((x // X_LOW) * Z_CHIPS + z, ((x % X_LOW) * Y_CHIPS + y) * 2 + core)


def along_z(cells, lane):
    left = jnp.where(lane == 0, 0.0, pltpu.roll(cells, 1, 1))
    right = jnp.where(lane == 127, 0.0, pltpu.roll(cells, 127, 1))
    return right + left


def along_y(cells, low_row, high_row, sub):
    low = jnp.where(sub == 0, jnp.broadcast_to(low_row, (8, 128)), pltpu.roll(cells, 1, 0))
    high = jnp.where(sub == 7, jnp.broadcast_to(high_row, (8, 128)), pltpu.roll(cells, 7, 0))
    return high + low


def slab_tendency(slab, beside, diffusivity, coupling):
    out = []
    for f in range(len(slab)):
        total = coupling[f, 0] * slab[0]
        for g in range(1, len(slab)):
            total = total + coupling[f, g] * slab[g]
        out.append(diffusivity[f] * (beside[f] - 6.0 * slab[f]) + total)
    return out


def split3(x):
    high = x.astype(BF16)
    rest = x - high.astype(F32)
    mid = rest.astype(BF16)
    low = (rest - mid.astype(F32)).astype(BF16)
    return high, mid, low


def dot_rows(a, b):
    return lax.dot_general(a, b, (((1,), (1,)), ((), ())), preferred_element_type=F32)


def dot_columns(a, b):
    return lax.dot_general(a, b, (((0,), (0,)), ((), ())), preferred_element_type=F32)


def eliminate(rows, col0):
    size, width = rows.shape
    count = size // 8
    tiles = width // 128
    values = [rows[8 * v:8 * v + 8] for v in range(count)]
    pivots = [jnp.zeros((8, 128), F32) for _ in range(count)]
    sub = lax.broadcasted_iota(jnp.int32, (8, 128), 0)
    for start in range(0, size, GROUP):
        v0 = start // 8
        spread = [
            [jnp.broadcast_to(values[v][:, col0 + start + p:col0 + start + p + 1], (8, 128)) for v in range(v0, count)]
            for p in range(GROUP)
        ]
        for p in range(GROUP):
            vp, s = (start + p) // 8, (start + p) % 8
            raw = spread[p]
            pivot = jnp.broadcast_to(raw[vp - v0][s:s + 1, :], (8, 128))
            inverse = 1.0 / pivot
            pivots[vp] = jnp.where(sub == s, pivot, pivots[vp])
            factors = {}
            for v in range(vp, count):
                factor = raw[v - v0] * inverse
                factors[v] = jnp.where(sub > s, factor, 0.0) if v == vp else factor
            for later in range(p + 1, GROUP):
                vl, sl = (start + later) // 8, (start + later) % 8
                across = jnp.broadcast_to(raw[vl - v0][sl:sl + 1, :], (8, 128))
                for v in range(vp, count):
                    spread[later][v - v0] = spread[later][v - v0] - factors[v] * across
            row = jnp.broadcast_to(values[vp][s:s + 1, :], (8, width))
            for v in range(vp, count):
                if v == vp and s == 7:
                    continue
                values[v] = values[v] - jnp.concatenate([factors[v]] * tiles, axis=1) * row
    return jnp.concatenate(
        [values[v] * jnp.concatenate([lax.rsqrt(pivots[v])] * tiles, axis=1) for v in range(count)], axis=0
    )


def pack_left(x, axis):
    h, m, l = split3(x)
    return jnp.concatenate([h, h, m, m, h, l], axis=axis)


def pack_right(x, axis):
    h, m, l = split3(x)
    return jnp.concatenate([h, m, h, m, l, h], axis=axis)


def eliminate_half(work, ends, store, between):
    b0 = 0
    rows = work[0:ends[0], :]
    for index, b1 in enumerate(ends):
        done = eliminate(rows, b0)
        i = lax.broadcasted_iota(jnp.int32, (b1 - b0, HALF), 0) + b0
        j = lax.broadcasted_iota(jnp.int32, (b1 - b0, HALF), 1)
        upper = jnp.where(j >= i, done[:, :HALF], 0.0)
        store(b0, b1, upper, done[:, HALF:])
        if index + 1 < len(ends):
            b2 = ends[index + 1]
            left = pack_left(upper, 0)
            right = pack_right(done, 0)
            rows = work[b1:b2, :] - dot_columns(left[:, b1:b2], right)
            if index + 2 < len(ends):
                b3 = ends[-1]
                work[b2:b3, :] = work[b2:b3, :] - dot_columns(left[:, b2:b3], right)
        between(index)
        b0 = b1


def gather_kernel(
    edges, total_rows,
    hist_ref, fields_ref, levels_ref, diff_ref, coup_ref,
    inverse_ref, upper_ref, snap, fine,
    hist, newest, fields, diff, coup,
    edge_sect, edge_blk, edge_corner, stage_blk, block,
    p_send, p_half, p_slots, p_part, p_final,
    h_send, h_half, h_slots, h_part, h_final,
    f_send, f_half, f_slots, f_part, f_final,
    work, work2,
    local_sem, send_sem, recv_sem,
):
    n_sect, n_blk = edges
    sect = lax.axis_index("sect")
    blk = lax.axis_index("blk")
    x, y, z, core = position()
    other = device(x, y, z, 1 - core)
    over_x = [device((x + k) % RING, y, z, core) for k in range(1, RING)]
    over_y = [device(x, (y + k) % RING, z, core) for k in range(1, RING)]
    over_z = [device(x, y, (z + k) % RING, core) for k in range(1, RING)]
    over = [over_x, over_y, over_z]
    sects = [(sect + n_sect - 1) % n_sect, (sect + 1) % n_sect]
    blks = [(blk + n_blk - 1) % n_blk, (blk + 1) % n_blk]
    sect_beside = [(s, blk) for s in sects]
    blk_beside = [(sect, b) for b in blks]
    corners = [[(s, b) for b in blks] for s in sects]
    peers = [other] + over_x + over_y + over_z + sect_beside + blk_beside + corners[0] + corners[1]

    count = fields_ref.shape[0]
    stored = hist_ref.shape[0]
    columns = stored + 2 * count
    scale = math.sqrt(total_rows)

    loads = [
        pltpu.make_async_copy(hist_ref.at[0:HALF], hist.at[0:HALF], local_sem.at[0]),
        pltpu.make_async_copy(fields_ref, fields, local_sem.at[1]),
        pltpu.make_async_copy(hist_ref.at[HALF:stored], hist.at[HALF:stored], local_sem.at[2]),
        pltpu.make_async_copy(diff_ref, diff, local_sem.at[3]),
        pltpu.make_async_copy(coup_ref, coup, local_sem.at[4]),
    ]
    for load in loads:
        load.start()
    barrier = pltpu.get_barrier_semaphore()
    for peer in peers:
        pl.semaphore_signal(barrier, inc=1, device_id=peer, device_id_type=MESH)

    def send(src, dst, index, target):
        pltpu.make_async_remote_copy(
            src_ref=src, dst_ref=dst, send_sem=send_sem.at[index], recv_sem=recv_sem.at[index],
            device_id=target, device_id_type=MESH,
        ).start()

    def wait_recv(ref, index):
        pltpu.make_async_copy(ref, ref, recv_sem.at[index]).wait()

    def wait_send(ref, index):
        pltpu.make_async_copy(ref, ref, send_sem.at[index]).wait()

    sub = lax.broadcasted_iota(jnp.int32, (8, 128), 0)
    lane = lax.broadcasted_iota(jnp.int32, (8, 128), 1)

    loads[1].wait()
    cells = [[fields[f, k] for k in range(2)] for f in range(count)]

    refined = (jnp.zeros((8, 128), jnp.int32) + levels_ref[0, 0]).astype(F32)
    for f in range(count):
        for k in range(2):
            block[2 * f + k] = cells[f][k]
            for side, (near, far) in enumerate(((0, 1), (7, 6))):
                stage_blk[side, k, f:f + 1, :] = cells[f][k][near:near + 1, :]
                stage_blk[side, 2 + k, f:f + 1, :] = cells[f][k][far:far + 1, :]
    block[2 * count] = refined
    for side in range(2):
        stage_blk[side, 4] = refined

    pl.semaphore_wait(barrier, len(peers))
    for side in range(2):
        send(block, edge_sect.at[1 - side], 0, sect_beside[side])
        send(stage_blk.at[side], edge_blk.at[1 - side], 1, blk_beside[side])
        for up in range(2):
            send(stage_blk.at[up, side], edge_corner.at[1 - side, 1 - up], 2, corners[side][up])

    local = snap.shape[1]
    loads[0].wait()
    first = hist[0:HALF].reshape(HALF, local)
    snap[0:HALF, :] = first
    square = dot_rows(first, first)
    third = HALF // 8
    for part in range(3):
        p_send[0, part] = square[third * part:third * part + third, :]
    p_send[1, 0] = square[3 * third:4 * third, :]
    corner = jnp.concatenate([square[64:96, 64:], square[96:128, 64:]], axis=1)
    p_send[1, 1] = corner[0:16]
    p_send[1, 2] = corner[16:32]
    send(p_send.at[1 - core], p_half, 4, other)

    loads[2].wait()
    second = jnp.concatenate(
        [hist[HALF:stored].reshape(stored - HALF, local), jnp.zeros((2 * count, local), BF16)], axis=0
    )
    snap[HALF:columns, :] = second
    h_send[0] = dot_rows(first, second).reshape(RING, 16, 128)
    h_send[1] = dot_rows(second, second).reshape(RING, 16, 128)
    send(h_send.at[1 - core], h_half.at[0], 5, other)

    def p_phase(phase):
        for k in range(RING - 1):
            for part in range(3):
                send(p_part.at[phase, part], p_slots.at[phase, part, k], 6 + phase, over[(part + phase) % 3][k])

    def p_sum(phase):
        wait_recv(p_slots.at[phase], 6 + phase)
        total = p_part[phase]
        for k in range(RING - 1):
            total = total + p_slots[phase, :, k]
        return total

    def total_of(own, slots):
        for k in range(RING - 1):
            own = own + slots[k]
        return own

    wait_recv(p_half, 4)
    p_part[0] = p_send[core] + p_half[...]
    p_phase(0)

    wait_recv(h_half.at[0], 5)
    h_half[1] = h_send[core] + h_half[0]
    for k in range(1, RING):
        send(h_half.at[1, (y + k) % RING], h_slots.at[0, k - 1], 9, over_y[k - 1])

    p_part[1] = p_sum(0)
    p_phase(1)

    wait_recv(h_slots.at[0], 9)
    h_part[0] = total_of(h_half[1, y], h_slots[0])
    for k in range(1, RING):
        send(h_part.at[0], h_slots.at[1, k - 1], 10, over_x[k - 1])

    for load in loads[3:]:
        load.wait()
    diffusivity = [jnp.broadcast_to(diff[0:1, f:f + 1], (8, 128)) for f in range(count)]
    coupling = {
        (f, g): jnp.broadcast_to(coup[f:f + 1, g:g + 1], (8, 128)) for f in range(count) for g in range(count)
    }
    spare = [jnp.zeros((8 - count, 128), F32)]
    diffusivity_rows = jnp.concatenate([diffusivity[f][0:1] for f in range(count)] + spare, axis=0)
    coupling_rows = [
        jnp.concatenate([coupling[f, g][0:1] for f in range(count)] + spare, axis=0) for g in range(count)
    ]
    wait_recv(edge_sect, 0)
    wait_recv(edge_blk, 1)
    wait_recv(edge_corner, 2)
    sect_out = [sect == 0, sect == n_sect - 1]
    blk_out = [blk == 0, blk == n_blk - 1]

    def inside(out, value):
        return jnp.where(out, 0.0, value)

    corner_rows = [
        [inside(sect_out[a] | blk_out[b], edge_corner[a, b]) for b in range(2)] for a in range(2)
    ]
    near = [[inside(blk_out[b], edge_blk[b, k]) for k in range(2)] for b in range(2)]
    far = [[inside(blk_out[b], edge_blk[b, 2 + k]) for k in range(2)] for b in range(2)]
    slabs = [
        [inside(sect_out[0], edge_sect[0, 2 * f]) for f in range(count)],
        [inside(sect_out[0], edge_sect[0, 2 * f + 1]) for f in range(count)],
        [cells[f][0] for f in range(count)],
        [cells[f][1] for f in range(count)],
        [inside(sect_out[1], edge_sect[1, 2 * f]) for f in range(count)],
        [inside(sect_out[1], edge_sect[1, 2 * f + 1]) for f in range(count)],
    ]
    strides = [1.0 / (1.0 + edge_sect[0, 2 * count]), None, None, 1.0 / (1.0 + edge_sect[1, 2 * count])]
    stride = 1.0 / (1.0 + refined)
    strides[1] = strides[2] = stride
    low_rows = [corner_rows[0][0], near[0][0], near[0][1], corner_rows[1][0]]
    high_rows = [corner_rows[0][1], near[1][0], near[1][1], corner_rows[1][1]]
    first_slabs = []
    for n in range(4):
        slab = slabs[n + 1]
        beside = [
            slabs[n][f] + slabs[n + 2][f] + along_z(slab[f], lane)
            + along_y(slab[f], low_rows[n][f:f + 1], high_rows[n][f:f + 1], sub)
            for f in range(count)
        ]
        tend = slab_tendency(slab, beside, diffusivity, coupling)
        first_slabs.append([slab[f] + strides[n] * tend[f] for f in range(count)])
    first_slabs[0] = [inside(sect_out[0], tile) for tile in first_slabs[0]]
    first_slabs[3] = [inside(sect_out[1], tile) for tile in first_slabs[3]]
    first_rows = []
    for b in range(2):
        stride_rows = 1.0 / (1.0 + edge_blk[b, 4])
        beside_rows = [corner_rows[0][b], near[b][0], near[b][1], corner_rows[1][b]]
        sides = []
        for k in range(2):
            rows = near[b][k]
            beside = beside_rows[k] + beside_rows[k + 2] + far[b][k] + stage_blk[b, k] + along_z(rows, lane)
            tend = diffusivity_rows * (beside - 6.0 * rows)
            for g in range(count):
                tend = tend + coupling_rows[g] * jnp.broadcast_to(rows[g:g + 1], (8, 128))
            sides.append(inside(blk_out[b], rows + stride_rows * tend))
        first_rows.append(sides)

    weight = refined * stride
    for k in range(2):
        slab = first_slabs[k + 1]
        beside = [
            first_slabs[k][f] + first_slabs[k + 2][f] + along_z(slab[f], lane)
            + along_y(slab[f], first_rows[0][k][f:f + 1], first_rows[1][k][f:f + 1], sub)
            for f in range(count)
        ]
        tend = slab_tendency(slab, beside, diffusivity, coupling)
        for f in range(count):
            final = slab[f] + weight * tend[f]
            newest[TAIL - 2 * count + f, k] = final
            newest[TAIL - count + f, k] = final - cells[f][k]
    newest[0:TAIL - 2 * count] = hist[columns - TAIL:stored].astype(F32)
    high, mid, low = split3(newest[...].reshape(TAIL, local))
    snap[columns - TAIL:columns, :] = high
    fine[0] = mid
    fine[1] = low
    pieces = jnp.concatenate([high, mid, low], axis=0)
    fresh = dot_rows(pieces, snap[...])
    fresh_fine = dot_rows(pieces, pieces[TAIL:])
    fresh = fresh[0:TAIL] + fresh[TAIL:2 * TAIL] + fresh[2 * TAIL:]
    extra = fresh_fine[0:TAIL, 0:TAIL] + (fresh_fine[0:TAIL, TAIL:] + fresh_fine[TAIL:2 * TAIL, 0:TAIL])
    f_send[0] = fresh[:, :HALF]
    f_send[1] = fresh[:, HALF:]
    f_send[1, :, HALF - TAIL:] = fresh[:, columns - TAIL:] + extra
    send(f_send.at[1 - core], f_half.at[0], 12, other)

    wait_recv(f_half.at[0], 12)
    f_part[0] = f_send[core] + f_half[0]
    for k in range(1, RING):
        send(f_part.at[0], f_slots.at[0, k - 1], 13, over_y[k - 1])

    p_part[2] = p_sum(1)
    p_phase(2)

    wait_recv(h_slots.at[1], 10)
    h_part[1] = total_of(h_part[0], h_slots[1])
    for k in range(1, RING):
        send(h_part.at[1], h_slots.at[2, k - 1], 11, over_z[k - 1])

    wait_recv(f_slots.at[0], 13)
    f_part[1] = total_of(f_part[0], f_slots[0])
    for k in range(1, RING):
        send(f_part.at[1], f_slots.at[1, k - 1], 16, over_x[k - 1])

    p_final[core] = p_sum(2)
    send(p_final.at[core], p_final.at[core], 14, other)

    wait_recv(h_slots.at[2], 11)
    h_final[core, y] = total_of(h_part[1], h_slots[2])
    for k in range(1, RING):
        send(h_final.at[core, y], h_final.at[core, y], 15, over_y[k - 1])

    wait_recv(p_final.at[0], 14)

    i = lax.broadcasted_iota(jnp.int32, (HALF, HALF), 0)
    j = lax.broadcasted_iota(jnp.int32, (HALF, HALF), 1)
    identity = (i == j).astype(F32)
    for part in range(3):
        work[16 * part:16 * part + 16, 0:HALF] = p_final[0, part]
    work[48:64, 0:HALF] = p_final[1, 0]
    lower = jnp.concatenate([p_final[1, 1], p_final[1, 2]], axis=0)
    work[64:96, 0:HALF] = jnp.concatenate([jnp.zeros((32, 64), F32), lower[:, :64]], axis=1)
    work[96:128, 0:HALF] = jnp.concatenate([jnp.zeros((32, 64), F32), lower[:, 64:]], axis=1)
    work[:, HALF:] = identity
    inverse_ref[0:HALF, HALF:] = jnp.zeros((HALF, HALF), F32)
    inverse_ref[columns - TAIL:, :] = jnp.zeros((TAIL, columns), F32)
    upper_ref[HALF:, 0:HALF] = jnp.zeros((HALF, HALF), F32)

    def store_first(b0, b1, upper, solved):
        upper_ref[b0:b1, 0:HALF] = upper * (1.0 / scale)
        inverse_ref[b0:b1, 0:HALF] = solved

    def between_first(index):
        if index == 1:
            wait_recv(f_slots.at[1], 16)
            f_part[2] = total_of(f_part[1], f_slots[1])
            for k in range(1, RING):
                send(f_part.at[2], f_slots.at[2, k - 1], 18, over_z[k - 1])

    eliminate_half(work, [32, 64, 96, 128], store_first, between_first)

    wait_recv(h_slots.at[2], 15)
    send(h_final.at[core], h_final.at[core], 17, other)
    wait_recv(h_final.at[0], 17)

    solved = inverse_ref[0:HALF, 0:HALF]
    side = jnp.dot(
        pack_left(solved, 1), pack_right(h_final[0].reshape(HALF, HALF), 0), preferred_element_type=F32
    )
    product = dot_columns(pack_left(side, 0), pack_right(jnp.concatenate([side, solved], axis=1), 0))
    work2[:, 0:HALF] = h_final[1].reshape(HALF, HALF) - product[:, :HALF]
    work2[:, HALF:2 * HALF] = -product[:, HALF:]
    work2[:, 2 * HALF:] = identity
    upper_ref[0:HALF, HALF:] = side * (1.0 / scale)

    def store_second(b0, b1, upper, solved):
        upper_ref[HALF + b0:HALF + b1, HALF:] = upper * (1.0 / scale)
        inverse_ref[HALF + b0:HALF + b1, :] = solved

    def between_second(index):
        if index == 2:
            wait_recv(f_slots.at[2], 18)
            f_final[core] = total_of(f_part[2], f_slots[2])
            send(f_final.at[core], f_final.at[core], 19, other)

    eliminate_half(work2, [32, 64, 96, HALF - TAIL], store_second, between_second)

    wait_recv(f_final.at[0], 19)
    row = lax.broadcasted_iota(jnp.int32, (TAIL, columns), 0)
    col = lax.broadcasted_iota(jnp.int32, (TAIL, columns), 1)
    last = jnp.concatenate([f_final[0], f_final[1]], axis=1)
    solved = inverse_ref[...]
    below = dot_rows(
        pack_left(jnp.where(col < columns - TAIL, last, 0.0), 1), pack_right(solved, 1)
    )
    left = pack_left(below, 1)
    placed = jnp.concatenate([jnp.zeros((HALF - TAIL, columns), F32), below], axis=0)
    rest = last[:, HALF:] - dot_rows(left, pack_right(placed, 1))
    onward = (col == row + (columns - TAIL)).astype(F32) - jnp.dot(
        left, pack_right(solved, 0), preferred_element_type=F32
    )
    done = eliminate(jnp.concatenate([rest, onward], axis=1), HALF - TAIL)
    inverse_ref[columns - TAIL:, :] = done[:, HALF:]
    turned = placed.T
    right_lanes = lax.broadcasted_iota(jnp.int32, (columns - TAIL, HALF), 1) >= HALF - TAIL
    upper_ref[0:columns - TAIL, HALF:] = jnp.where(
        right_lanes, turned[0:columns - TAIL] * (1.0 / scale), upper_ref[0:columns - TAIL, HALF:]
    )
    row = lax.broadcasted_iota(jnp.int32, (TAIL, HALF), 0)
    col = lax.broadcasted_iota(jnp.int32, (TAIL, HALF), 1)
    upper_ref[columns - TAIL:, HALF:] = jnp.where(
        col >= row + (HALF - TAIL), done[:, :HALF] * (1.0 / scale), 0.0
    )

    wait_send(edge_sect, 0)
    wait_send(edge_blk, 1)
    wait_send(edge_corner, 2)
    wait_send(p_half, 4)
    wait_send(h_half.at[0], 5)
    for phase in range(3):
        wait_send(p_slots.at[phase], 6 + phase)
        wait_send(h_slots.at[phase], 9 + phase)
    wait_send(f_half.at[0], 12)
    wait_send(f_slots.at[0], 13)
    wait_send(p_final.at[0], 14)
    wait_send(h_slots.at[0], 15)
    wait_send(f_slots.at[1], 16)
    wait_send(h_final.at[0], 17)
    wait_send(f_slots.at[2], 18)
    wait_send(f_final.at[0], 19)


def finish_kernel(
    total_rows,
    inverse_ref, upper_ref, snap, fine,
    modes_ref, factor_ref,
    modes, local_sem,
):
    size = inverse_ref.shape[0]
    scale = math.sqrt(total_rows)
    keep = pltpu.make_async_copy(upper_ref, factor_ref, local_sem.at[0])
    keep.start()
    step = 128
    stores = []
    tail = jnp.concatenate([fine[0], fine[0], fine[0], fine[1]], axis=0)
    for r0 in range(0, size, step):
        h, m, l = split3(inverse_ref[r0:r0 + step, :] * scale)
        left = jnp.concatenate([h, m, l], axis=0)
        last = jnp.concatenate(
            [h[:, size - TAIL:], m[:, size - TAIL:], l[:, size - TAIL:], h[:, size - TAIL:]], axis=1
        )
        for c in range(0, snap.shape[1], 256):
            out = jnp.dot(left, snap[:, c:c + 256], preferred_element_type=F32)
            out = (out[:step] + out[step:2 * step]) + out[2 * step:]
            out = out + jnp.dot(last, tail[:, c:c + 256], preferred_element_type=F32)
            for q in range(2):
                modes[pl.ds(r0 * 16 + c // 128 + q, step, stride=16), :] = out[:, 128 * q:128 * q + 128]
        store = pltpu.make_async_copy(
            modes.at[pl.ds(r0 * 16, step * 16)], modes_ref.at[pl.ds(r0 * 16, step * 16)], local_sem.at[1 + r0 // step]
        )
        store.start()
        stores.append(store)
    keep.wait()
    for store in stores:
        store.wait()


def in_hbm(array):
    return pltpu.with_memory_space_constraint(array, pltpu.HBM)


def shards(fields, history, levels, diffusivity, coupling):
    edges = (lax.axis_size("sect"), lax.axis_size("blk"))
    stored, count_x, count_y, count_z = history.shape
    count = fields.shape[0]
    columns = stored + 2 * count
    local = count_x * count_y * count_z
    total_rows = local * edges[0] * edges[1]
    vmem = pl.BlockSpec(memory_space=pltpu.VMEM)
    hbm = pl.BlockSpec(memory_space=pltpu.HBM)
    smem = pl.BlockSpec(memory_space=pltpu.SMEM)
    tile = (16, 128)
    inverse, upper, snap, fine = pl.pallas_call(
        functools.partial(gather_kernel, edges, total_rows),
        out_shape=[
            jax.ShapeDtypeStruct((columns, columns), F32),
            jax.ShapeDtypeStruct((columns, columns), F32),
            jax.ShapeDtypeStruct((columns, local), BF16),
            jax.ShapeDtypeStruct((2, TAIL, local), BF16),
        ],
        in_specs=[hbm, hbm, smem, hbm, hbm],
        out_specs=[vmem, vmem, vmem, vmem],
        scratch_shapes=[
            pltpu.VMEM(history.shape, BF16),
            pltpu.VMEM((TAIL,) + history.shape[1:], F32),
            pltpu.VMEM(fields.shape, F32),
            pltpu.VMEM((1, count), F32),
            pltpu.VMEM((count, count), F32),
            pltpu.VMEM((2, 2 * count + 1, 8, 128), F32),
            pltpu.VMEM((2, 5, 8, 128), F32),
            pltpu.VMEM((2, 2, 8, 128), F32),
            pltpu.VMEM((2, 5, 8, 128), F32),
            pltpu.VMEM((2 * count + 1, 8, 128), F32),
            pltpu.VMEM((2, 3) + tile, F32),
            pltpu.VMEM((3,) + tile, F32),
            pltpu.VMEM((3, 3, RING - 1) + tile, F32),
            pltpu.VMEM((3, 3) + tile, F32),
            pltpu.VMEM((2, 3) + tile, F32),
            pltpu.VMEM((2, RING) + tile, F32),
            pltpu.VMEM((2, RING) + tile, F32),
            pltpu.VMEM((3, RING - 1) + tile, F32),
            pltpu.VMEM((2,) + tile, F32),
            pltpu.VMEM((2, RING) + tile, F32),
            pltpu.VMEM((2,) + tile, F32),
            pltpu.VMEM((1,) + tile, F32),
            pltpu.VMEM((3, RING - 1) + tile, F32),
            pltpu.VMEM((3,) + tile, F32),
            pltpu.VMEM((2,) + tile, F32),
            pltpu.VMEM((HALF, 2 * HALF), F32),
            pltpu.VMEM((HALF, 3 * HALF), F32),
            pltpu.SemaphoreType.DMA((5,)),
            pltpu.SemaphoreType.DMA((20,)),
            pltpu.SemaphoreType.DMA((20,)),
        ],
        compiler_params=pltpu.CompilerParams(
            collective_id=0, has_side_effects=True, vmem_limit_bytes=32 << 20
        ),
        name="gather",
    )(in_hbm(history), in_hbm(fields), levels, in_hbm(diffusivity.reshape(1, count)), in_hbm(coupling))
    modes, factor = pl.pallas_call(
        functools.partial(finish_kernel, total_rows),
        out_shape=[
            jax.ShapeDtypeStruct((columns * 16, 128), F32),
            jax.ShapeDtypeStruct((columns, columns), F32),
        ],
        in_specs=[vmem, vmem, vmem, vmem],
        out_specs=[hbm, hbm],
        scratch_shapes=[
            pltpu.VMEM((columns * 16, 128), F32),
            pltpu.SemaphoreType.DMA((5,)),
        ],
        compiler_params=pltpu.CompilerParams(vmem_limit_bytes=32 << 20),
        name="finish",
    )(inverse, upper, snap, fine)
    return modes.reshape(columns, count_x, count_y, count_z), factor


def solution(mesh):
    return jax.shard_map(
        shards,
        mesh=mesh,
        in_specs=(
            P(None, "sect", "blk", None),
            P(None, "sect", "blk", None),
            P("sect", "blk"),
            P(),
            P(),
        ),
        out_specs=(P(None, "sect", "blk", None), P()),
        check_vma=False,
    )
```
